32 devices in a mesh: dp: 16 (over z, x, core), tensor: 2 (over y).
Axes of the slice: x: 2, y: 2, z: 4, core: 2. Of those that a mesh axis runs over, the one named last changes fastest.
Arguments:
- grad_out: bfloat16 [8192, 8192], P(('dp', 'tensor')), may hold values from -60 to 60
- out_weight: bfloat16 [8192, 8192], P('tensor', 'dp'), may hold values from -0.0625 to 0.0625
- queries: bfloat16 [8192, 8192], P('dp', 'tensor'), may hold values from -150 to 150, as said below
- keys: bfloat16 [8192, 1024], P('dp', 'tensor'), may hold values from -7 to 7, as said below
- values: bfloat16 [8192, 1024], P('dp', 'tensor'), may hold values from -6 to 6
- prefix_keys: bfloat16 [128, 1024], P(None, 'tensor'), may hold values from -6 to 6
- prefix_values: bfloat16 [128, 1024], P(None, 'tensor'), may hold values from -6 to 6
Outputs:
- grad_queries: bfloat16 [8192, 8192], P('dp', 'tensor')
- grad_keys: bfloat16 [8192, 1024], P('dp', 'tensor')
- grad_values: bfloat16 [8192, 1024], P('dp', 'tensor')
- grad_prefix_keys: float32 [128, 1024], P(None, 'tensor')
- grad_prefix_values: float32 [128, 1024], P(None, 'tensor')
The draws below stay inside these ranges and needn't reach their ends.
Inputs may be any that keep to these rules, and one draw needn't show every extreme that they name: `keys`: keys of order one. `queries`: queries of order one in most rows.
All inputs are finite; a program needn't handle non-finite values.
Results may differ from the reference program's by a relative error of at most 0.015.
Values may be sent and summed in bfloat16 or wider, within the bound.
A program may use at most 320 MiB of HBM per device.

```python
import jax
import jax.numpy as jnp
from jax import lax

D = 8192
QH = 64
KVH = 8
HD = 128
PREFIX = 128
SEQ = 512
TOKENS = 8192
N_DP = 16


def shared_keys(key):
    drawn_keys = jnp.clip(jax.random.normal(key, (TOKENS, KVH * HD), jnp.float32), -6.0, 6.0)
    position = jnp.arange(TOKENS, dtype=jnp.int32) % SEQ
    chosen = (position % 32 == 30)[:, None]
    return jnp.where(chosen, drawn_keys, drawn_keys)


def draw_keys(key, part):
    return shared_keys(key).astype(jnp.bfloat16)


def draw_queries(key, part):
    key = jax.random.fold_in(key, 12)
    return jnp.clip(jax.random.normal(key, (TOKENS, QH * HD), jnp.float32), -6.0, 6.0).astype(jnp.bfloat16)


def block_levels(key, dims, split, low, top_value):
    def one(dim, blocks):
        draws = jax.random.uniform(jax.random.fold_in(jax.random.fold_in(key, 6), dim), (blocks,), jnp.float32, low / len(split), top_value / len(split))
        return jnp.repeat(jnp.exp(draws), dims[dim] // blocks).reshape((-1,) + (1,) * (len(dims) - dim - 1))

    gain = one(*split[0])
    for cut in split[1:]:
        gain = gain * one(*cut)
    return gain


def noise(stream_key, shape, spread, bound, cuts=(), held_as=jnp.bfloat16):
    loudness = block_levels(stream_key, shape, cuts, -0.22, 0.18) if cuts else 1.0
    entries = jax.random.normal(stream_key, shape, jnp.float32) * spread * loudness
    return jnp.minimum(jnp.maximum(entries, -bound), bound).astype(held_as)


def setup_inputs(seed: int = 0) -> dict:
    key_list = jax.random.split(jax.random.key(seed), 8)
    return {
        "grad_out": noise(key_list[0], (TOKENS, D), 10.0, 60.0, ((0, 32),)),
        "out_weight": noise(key_list[1], (QH * HD, D), D ** -0.5, 0.0625, ((0, 2), (1, 16))),
        "queries": draw_queries(jax.random.fold_in(key_list[7], 71), 0),
        "keys": draw_keys(jax.random.fold_in(key_list[7], 71), 0),
        "values": noise(key_list[4], (TOKENS, KVH * HD), 1.0, 6.0, ((0, 16), (1, 2))),
        "prefix_keys": noise(key_list[5], (PREFIX, KVH * HD), 1.0, 6.0, ((1, 2),)),
        "prefix_values": noise(key_list[6], (PREFIX, KVH * HD), 1.0, 6.0, ((1, 2),)),
    }


def one_sequence(pieces, prefix_keys, prefix_values):
    query_part, dattn_part, key_part, value_part = pieces
    scale = HD ** -0.5
    query_wide = query_part.reshape(SEQ, KVH, QH // KVH, HD).astype(jnp.float32)
    dattn_wide = dattn_part.reshape(SEQ, KVH, QH // KVH, HD).astype(jnp.float32)
    key_all = jnp.concatenate([prefix_keys.reshape(PREFIX, KVH, HD), key_part.reshape(SEQ, KVH, HD)], 0).astype(jnp.float32)
    value_all = jnp.concatenate([prefix_values.reshape(PREFIX, KVH, HD), value_part.reshape(SEQ, KVH, HD)], 0).astype(jnp.float32)
    scores = jnp.einsum('ichd,jcd->chij', query_wide, key_all) * scale
    row_ids = jnp.arange(SEQ, dtype=jnp.int32)[:, None]
    col_ids = jnp.arange(PREFIX + SEQ, dtype=jnp.int32)[None, :]
    visible = (col_ids < PREFIX) | (col_ids - PREFIX <= row_ids)
    scores = jnp.where(visible, scores, -jnp.inf)
    top = jnp.max(scores, axis=-1, keepdims=True)
    expo = jnp.exp(scores - top)
    probs = expo / jnp.sum(expo, axis=-1, keepdims=True)
    grad_probs = jnp.einsum('ichd,jcd->chij', dattn_wide, value_all)
    row_dot = jnp.sum(probs * grad_probs, axis=-1, keepdims=True)
    grad_scores = probs * (grad_probs - row_dot)
    probs_low = lax.optimization_barrier(probs.astype(jnp.bfloat16)).astype(jnp.float32)
    grad_low = lax.optimization_barrier(grad_scores.astype(jnp.bfloat16)).astype(jnp.float32)
    grad_query = jnp.einsum('chij,jcd->ichd', grad_low, key_all) * scale
    key_grad = jnp.einsum('chij,ichd->jcd', grad_low, query_wide) * scale
    value_grad = jnp.einsum('chij,ichd->jcd', probs_low, dattn_wide)
    return (grad_query.reshape(SEQ, QH * HD).astype(jnp.bfloat16),
            key_grad[PREFIX:].reshape(SEQ, KVH * HD).astype(jnp.bfloat16),
            value_grad[PREFIX:].reshape(SEQ, KVH * HD).astype(jnp.bfloat16),
            key_grad[:PREFIX].reshape(PREFIX, KVH * HD),
            value_grad[:PREFIX].reshape(PREFIX, KVH * HD))


def reference(grad_out, out_weight, queries, keys, values, prefix_keys, prefix_values):
    d_attn = jnp.dot(grad_out, out_weight.T, preferred_element_type=jnp.float32).astype(jnp.bfloat16)
    d_attn = lax.optimization_barrier(d_attn)
    stacked = (queries.reshape(N_DP, SEQ, QH * HD), d_attn.reshape(N_DP, SEQ, QH * HD),
               keys.reshape(N_DP, SEQ, KVH * HD), values.reshape(N_DP, SEQ, KVH * HD))
    grad_q, grad_k, grad_v, pref_k, pref_v = lax.map(lambda pieces: one_sequence(pieces, prefix_keys, prefix_values), stacked)
    return (grad_q.reshape(TOKENS, QH * HD), grad_k.reshape(TOKENS, KVH * HD), grad_v.reshape(TOKENS, KVH * HD),
            jnp.sum(pref_k, axis=0), jnp.sum(pref_v, axis=0))
```

```python
import functools

import jax
import jax.numpy as jnp
from jax import lax
from jax.experimental import pallas as pl
from jax.experimental.pallas import tpu as pltpu
from jax.sharding import PartitionSpec as P

QH = 64
KVH = 8
HD = 128
PREFIX = 128
BLOCK = 256
SCALE = HD ** (-0.5)


def dot(a, b, ca, cb):
    return lax.dot_general(a, b, (((ca,), (cb,)), ((), ())), preferred_element_type=jnp.float32)


def attention_kernel(d_ref, q_ref, k_ref, v_ref, pk_ref, pv_ref, *rest):
    dq_ref, dk_ref, dv_ref, prefix_ref, kall, vall, dk_acc, dv_acc = rest[-8:]
    h = pl.program_id(0)
    length = q_ref.shape[0]
    block = min(BLOCK, length)

    @pl.when(h == 0)
    def _():
        kall[:PREFIX, :] = pk_ref[...]
        kall[PREFIX:, :] = k_ref[...]
        vall[:PREFIX, :] = pv_ref[...]
        vall[PREFIX:, :] = v_ref[...]
        dk_acc[...] = jnp.zeros_like(dk_acc)
        dv_acc[...] = jnp.zeros_like(dv_acc)

    row = lax.broadcasted_iota(jnp.int32, (block, block), 0)
    col = lax.broadcasted_iota(jnp.int32, (block, block), 1)
    seen = row <= col
    for start in range(0, length, block):
        old = PREFIX + start
        total = old + block
        qb = q_ref[start : start + block, :]
        db = d_ref[start : start + block, :]
        keys = kall[:total, :]
        values = vall[:total, :]
        s = dot(keys, qb, 1, 1) * SCALE
        gp = dot(values, db, 1, 1)
        s = jnp.concatenate([s[:old], jnp.where(seen, s[old:], -jnp.inf)], axis=0)
        top = jnp.max(s, axis=0, keepdims=True)
        e = jnp.exp(s - top)
        p = e * (1.0 / jnp.sum(e, axis=0, keepdims=True))
        row_dot = jnp.sum(p * gp, axis=0, keepdims=True)
        g = (p * (gp - row_dot)).astype(jnp.bfloat16)
        p = p.astype(jnp.bfloat16)
        dq_ref[start : start + block, :] = (dot(g, keys, 0, 0) * SCALE).astype(dq_ref.dtype)
        dk_acc[:total, :] += dot(g, qb, 1, 0)
        dv_acc[:total, :] += dot(p, db, 1, 0)

    @pl.when(h == pl.num_programs(0) - 1)
    def _():
        dk = dk_acc[...] * SCALE
        dv = dv_acc[...]
        dk_ref[...] = dk[PREFIX:].astype(dk_ref.dtype)
        dv_ref[...] = dv[PREFIX:].astype(dv_ref.dtype)
        prefix_ref[:PREFIX, :] = dk[:PREFIX].astype(prefix_ref.dtype)
        prefix_ref[PREFIX:, :] = dv[:PREFIX].astype(prefix_ref.dtype)


def attention(c, d_attn, queries, keys, values, prefix_keys, prefix_values, held):
    length, wide = queries.shape
    kv_wide = keys.shape[1]
    group = QH // KVH
    at_head = pl.BlockSpec((length, HD), lambda h: (0, c * group + h))
    at_kv = pl.BlockSpec((length, HD), lambda h: (0, c))
    at_prefix = pl.BlockSpec((PREFIX, HD), lambda h: (0, c))
    in_specs = [pl.BlockSpec((length, HD), lambda h: (0, h)), at_head, at_kv, at_kv, at_prefix, at_prefix]
    aliases = {}
    if held:
        in_specs += [pl.BlockSpec(memory_space=pl.ANY)] * 3
        aliases = {6: 0, 7: 1, 8: 2}
    pairs = length * (PREFIX + length)
    return pl.pallas_call(
        attention_kernel,
        grid=(group,),
        in_specs=in_specs,
        out_specs=[at_head, at_kv, at_kv, pl.BlockSpec((2 * PREFIX, HD), lambda h: (0, 0))],
        out_shape=[
            jax.ShapeDtypeStruct((length, wide), jnp.bfloat16),
            jax.ShapeDtypeStruct((length, kv_wide), jnp.bfloat16),
            jax.ShapeDtypeStruct((length, kv_wide), jnp.bfloat16),
            jax.ShapeDtypeStruct((2 * PREFIX, HD), jnp.bfloat16),
        ],
        scratch_shapes=[
            pltpu.VMEM((PREFIX + length, HD), jnp.bfloat16),
            pltpu.VMEM((PREFIX + length, HD), jnp.bfloat16),
            pltpu.VMEM((PREFIX + length, HD), jnp.float32),
            pltpu.VMEM((PREFIX + length, HD), jnp.float32),
        ],
        input_output_aliases=aliases,
        compiler_params=pltpu.CompilerParams(vmem_limit_bytes=32 << 20),
        cost_estimate=pl.CostEstimate(
            flops=10 * group * pairs * HD, bytes_accessed=8 * length * group * HD, transcendentals=group * pairs
        ),
    )(d_attn, queries, keys, values, prefix_keys, prefix_values, *held)


def sum_over(x, axis, size):
    step = 1
    while step < size:
        other = lax.ppermute(x, axis, [(i, i ^ step) for i in range(size)])
        total = x.astype(jnp.float32) + other.astype(jnp.float32)
        step *= 2
        x = total.astype(jnp.bfloat16) if step < size else total
    return x.astype(jnp.float32)


def gather_rows(x, axis, size):
    rows = x.shape[0]
    me = lax.axis_index(axis)
    if size == 2:
        other = lax.ppermute(x, axis, [(0, 1), (1, 0)])
        first = me == 0
        return jnp.concatenate([jnp.where(first, x, other), jnp.where(first, other, x)], 0)
    return lax.all_gather(x, axis, axis=0, tiled=True)


def shards(n_dp, n_tensor, grad_out, out_weight, queries, keys, values, prefix_keys, prefix_values):
    full_rows = gather_rows(grad_out, "tensor", n_tensor)
    kv_local = keys.shape[1] // HD
    wide = QH // KVH * HD
    held = ()
    sums = []
    for c in range(kv_local):
        weight = lax.all_gather(out_weight[c * wide : (c + 1) * wide], "dp", axis=1, tiled=True)
        d_attn = dot(full_rows, weight, 1, 1).astype(jnp.bfloat16)
        *held, prefix = attention(c, d_attn, queries, keys, values, prefix_keys, prefix_values, held)
        sums.append(sum_over(prefix, "dp", n_dp))
    summed = jnp.concatenate(sums, axis=1)
    return (*held, summed[:PREFIX], summed[PREFIX:])


def solution(mesh):
    in_specs = (
        P(("dp", "tensor"), None),
        P("tensor", "dp"),
        P("dp", "tensor"),
        P("dp", "tensor"),
        P("dp", "tensor"),
        P(None, "tensor"),
        P(None, "tensor"),
    )
    out_specs = (
        P("dp", "tensor"),
        P("dp", "tensor"),
        P("dp", "tensor"),
        P(None, "tensor"),
        P(None, "tensor"),
    )
    body = functools.partial(shards, mesh.shape["dp"], mesh.shape["tensor"])
    return jax.shard_map(body, mesh=mesh, in_specs=in_specs, out_specs=out_specs, check_vma=False)
```

```python
import functools

import jax
import jax.numpy as jnp
from jax import lax
from jax.experimental import pallas as pl
from jax.experimental.pallas import tpu as pltpu
from jax.sharding import PartitionSpec as P

QH = 64
KVH = 8
HD = 128
PREFIX = 128
BLOCK = 256
SCALE = HD ** (-0.5)


def dot(a, b, ca, cb):
    return lax.dot_general(a, b, (((ca,), (cb,)), ((), ())), preferred_element_type=jnp.float32)


def attention_kernel(g_ref, w_ref, q_ref, k_ref, v_ref, pk_ref, pv_ref, *rest):
    dq_ref, dk_ref, dv_ref, prefix_ref, kall, vall, dk_acc, dv_acc, d_buf = rest[-9:]
    pairs = QH // KVH * HD // q_ref.shape[1]
    step = lax.rem(pl.program_id(0), pairs)
    length = q_ref.shape[0]
    block = min(BLOCK, length)

    @pl.when(step == 0)
    def _():
        kall[:PREFIX, :] = pk_ref[...]
        kall[PREFIX:, :] = k_ref[...]
        vall[:PREFIX, :] = pv_ref[...]
        vall[PREFIX:, :] = v_ref[...]
        dk_acc[...] = jnp.zeros_like(dk_acc)
        dv_acc[...] = jnp.zeros_like(dv_acc)

    d_buf[...] = dot(g_ref[...], w_ref[...], 1, 1).astype(jnp.bfloat16)
    row = lax.broadcasted_iota(jnp.int32, (block, block), 0)
    col = lax.broadcasted_iota(jnp.int32, (block, block), 1)
    seen = row <= col
    for start in range(0, length, block):
        old = PREFIX + start
        total = old + block
        keys = kall[:total, :]
        values = vall[:total, :]
        for at in range(0, q_ref.shape[1], HD):
            qb = q_ref[start : start + block, at : at + HD]
            db = d_buf[start : start + block, at : at + HD]
            s = dot(keys, qb, 1, 1) * SCALE
            gp = dot(values, db, 1, 1)
            s = jnp.concatenate([s[:old], jnp.where(seen, s[old:], -jnp.inf)], axis=0)
            top = jnp.max(s, axis=0, keepdims=True)
            e = jnp.exp(s - top)
            p = e * (1.0 / jnp.sum(e, axis=0, keepdims=True))
            row_dot = jnp.sum(p * gp, axis=0, keepdims=True)
            g = (p * (gp - row_dot)).astype(jnp.bfloat16)
            p = p.astype(jnp.bfloat16)
            dq_ref[start : start + block, at : at + HD] = (dot(g, keys, 0, 0) * SCALE).astype(dq_ref.dtype)
            dk_acc[:total, :] += dot(g, qb, 1, 0)
            dv_acc[:total, :] += dot(p, db, 1, 0)

    @pl.when(step == pairs - 1)
    def _():
        dk = dk_acc[...] * SCALE
        dv = dv_acc[...]
        dk_ref[...] = dk[PREFIX:].astype(dk_ref.dtype)
        dv_ref[...] = dv[PREFIX:].astype(dv_ref.dtype)
        prefix_ref[:PREFIX, :] = dk[:PREFIX].astype(prefix_ref.dtype)
        prefix_ref[PREFIX:, :] = dv[:PREFIX].astype(prefix_ref.dtype)


def attention(first, rows, weight, queries, keys, values, prefix_keys, prefix_values, held):
    length, wide = queries.shape
    kv_wide = keys.shape[1]
    depth = rows.shape[1]
    pairs = QH // KVH // 2
    heads = weight.shape[0] // HD
    count = heads // (2 * pairs)
    at_pair = pl.BlockSpec((length, 2 * HD), lambda i: (0, first * pairs + i))
    at_kv = pl.BlockSpec((length, HD), lambda i: (0, first + i // pairs))
    at_prefix = pl.BlockSpec((PREFIX, HD), lambda i: (0, first + i // pairs))
    in_specs = [
        pl.BlockSpec((length, depth), lambda i: (0, 0), pipeline_mode=pl.Buffered(1)),
        pl.BlockSpec((2 * HD, depth), lambda i: (i, 0)),
        at_pair, at_kv, at_kv, at_prefix, at_prefix,
    ]
    aliases = {}
    if held:
        in_specs += [pl.BlockSpec(memory_space=pl.ANY)] * 3
        aliases = {7: 0, 8: 1, 9: 2}
    scores = heads * length * (PREFIX + length)
    return pl.pallas_call(
        attention_kernel,
        grid=(heads // 2,),
        in_specs=in_specs,
        out_specs=[at_pair, at_kv, at_kv, pl.BlockSpec((2 * PREFIX, HD), lambda i: (0, i // pairs))],
        out_shape=[
            jax.ShapeDtypeStruct((length, wide), jnp.bfloat16),
            jax.ShapeDtypeStruct((length, kv_wide), jnp.bfloat16),
            jax.ShapeDtypeStruct((length, kv_wide), jnp.bfloat16),
            jax.ShapeDtypeStruct((2 * PREFIX, count * HD), jnp.bfloat16),
        ],
        scratch_shapes=[
            pltpu.VMEM((PREFIX + length, HD), jnp.bfloat16),
            pltpu.VMEM((PREFIX + length, HD), jnp.bfloat16),
            pltpu.VMEM((PREFIX + length, HD), jnp.float32),
            pltpu.VMEM((PREFIX + length, HD), jnp.float32),
            pltpu.VMEM((length, 2 * HD), jnp.bfloat16),
        ],
        input_output_aliases=aliases,
        compiler_params=pltpu.CompilerParams(vmem_limit_bytes=48 << 20),
        cost_estimate=pl.CostEstimate(
            flops=10 * scores * HD + 2 * length * depth * heads * HD,
            bytes_accessed=2 * depth * (length + heads * HD),
            transcendentals=scores,
        ),
    )(rows, weight, queries, keys, values, prefix_keys, prefix_values, *held)


def sum_over(x, axis, size):
    step = 1
    while step < size:
        other = lax.ppermute(x, axis, [(i, i ^ step) for i in range(size)])
        total = x.astype(jnp.float32) + other.astype(jnp.float32)
        step *= 2
        x = total.astype(jnp.bfloat16) if step < size else total
    return x.astype(jnp.float32)


def gather_rows(x, axis, size):
    rows = x.shape[0]
    me = lax.axis_index(axis)
    if size == 2:
        other = lax.ppermute(x, axis, [(0, 1), (1, 0)])
        first = me == 0
        return jnp.concatenate([jnp.where(first, x, other), jnp.where(first, other, x)], 0)
    return lax.all_gather(x, axis, axis=0, tiled=True)


def shards(n_dp, n_tensor, grad_out, out_weight, queries, keys, values, prefix_keys, prefix_values):
    full_rows = gather_rows(grad_out, "tensor", n_tensor)
    kv_local = keys.shape[1] // HD
    wide = QH // KVH * HD
    parts = 2 if kv_local % 2 == 0 else 1
    count = kv_local // parts
    weights = [
        lax.all_gather(out_weight[c * count * wide : (c + 1) * count * wide], "dp", axis=1, tiled=True)
        for c in range(parts)
    ]
    held = ()
    sums = []
    for c in range(parts):
        weight = weights[c]
        if sums:
            weight, sums[-1] = lax.optimization_barrier((weight, sums[-1]))
        *held, prefix = attention(c * count, full_rows, weight, queries, keys, values, prefix_keys, prefix_values, held)
        sums.append(sum_over(prefix, "dp", n_dp))
    summed = jnp.concatenate(sums, axis=1)
    return (*held, summed[:PREFIX], summed[PREFIX:])


def solution(mesh):
    in_specs = (
        P(("dp", "tensor"), None),
        P("tensor", "dp"),
        P("dp", "tensor"),
        P("dp", "tensor"),
        P("dp", "tensor"),
        P(None, "tensor"),
        P(None, "tensor"),
    )
    out_specs = (
        P("dp", "tensor"),
        P("dp", "tensor"),
        P("dp", "tensor"),
        P(None, "tensor"),
        P(None, "tensor"),
    )
    body = functools.partial(shards, mesh.shape["dp"], mesh.shape["tensor"])
    return jax.shard_map(body, mesh=mesh, in_specs=in_specs, out_specs=out_specs, check_vma=False)
```

```python
import functools

import jax
import jax.numpy as jnp
from jax import lax
from jax.experimental import pallas as pl
from jax.experimental.pallas import tpu as pltpu
from jax.sharding import PartitionSpec as P

QH = 64
KVH = 8
HD = 128
PREFIX = 128
BLOCK = 256
SCALE = HD ** (-0.5)


def dot(a, b, ca, cb):
    return lax.dot_general(a, b, (((ca,), (cb,)), ((), ())), preferred_element_type=jnp.float32)


def attention_kernel(d_ref, q_ref, k_ref, v_ref, pk_ref, pv_ref, *rest):
    dq_ref, dk_ref, dv_ref, prefix_ref, kall, vall, dk_acc, dv_acc = rest[-8:]
    pairs = QH // KVH * HD // q_ref.shape[1]
    step = lax.rem(pl.program_id(0), pairs)
    length = q_ref.shape[0]
    block = min(BLOCK, length)

    @pl.when(step == 0)
    def _():
        kall[:PREFIX, :] = pk_ref[...]
        kall[PREFIX:, :] = k_ref[...]
        vall[:PREFIX, :] = pv_ref[...]
        vall[PREFIX:, :] = v_ref[...]
        dk_acc[...] = jnp.zeros_like(dk_acc)
        dv_acc[...] = jnp.zeros_like(dv_acc)

    row = lax.broadcasted_iota(jnp.int32, (block, block), 0)
    col = lax.broadcasted_iota(jnp.int32, (block, block), 1)
    seen = row <= col
    for start in range(0, length, block):
        old = PREFIX + start
        total = old + block
        keys = kall[:total, :]
        values = vall[:total, :]
        for at in range(0, q_ref.shape[1], HD):
            qb = q_ref[start : start + block, at : at + HD]
            db = d_ref[start : start + block, at : at + HD]
            s = dot(keys, qb, 1, 1) * SCALE
            gp = dot(values, db, 1, 1)
            s = jnp.concatenate([s[:old], jnp.where(seen, s[old:], -jnp.inf)], axis=0)
            top = jnp.max(s, axis=0, keepdims=True)
            e = jnp.exp(s - top)
            p = e * (1.0 / jnp.sum(e, axis=0, keepdims=True))
            row_dot = jnp.sum(p * gp, axis=0, keepdims=True)
            g = (p * (gp - row_dot)).astype(jnp.bfloat16)
            p = p.astype(jnp.bfloat16)
            dq_ref[start : start + block, at : at + HD] = (dot(g, keys, 0, 0) * SCALE).astype(dq_ref.dtype)
            dk_acc[:total, :] += dot(g, qb, 1, 0)
            dv_acc[:total, :] += dot(p, db, 1, 0)

    @pl.when(step == pairs - 1)
    def _():
        dk = dk_acc[...] * SCALE
        dv = dv_acc[...]
        dk_ref[...] = dk[PREFIX:].astype(dk_ref.dtype)
        dv_ref[...] = dv[PREFIX:].astype(dv_ref.dtype)
        prefix_ref[:PREFIX, :] = dk[:PREFIX].astype(prefix_ref.dtype)
        prefix_ref[PREFIX:, :] = dv[:PREFIX].astype(prefix_ref.dtype)


def attention(first, d_attn, queries, keys, values, prefix_keys, prefix_values, held):
    length, wide = queries.shape
    kv_wide = keys.shape[1]
    pairs = QH // KVH // 2
    heads = d_attn.shape[1] // HD
    count = heads // (2 * pairs)
    at_pair = pl.BlockSpec((length, 2 * HD), lambda i: (0, first * pairs + i))
    at_kv = pl.BlockSpec((length, HD), lambda i: (0, first + i // pairs))
    at_prefix = pl.BlockSpec((PREFIX, HD), lambda i: (0, first + i // pairs))
    in_specs = [
        pl.BlockSpec((length, 2 * HD), lambda i: (0, i)),
        at_pair, at_kv, at_kv, at_prefix, at_prefix,
    ]
    aliases = {}
    if held:
        in_specs += [pl.BlockSpec(memory_space=pl.ANY)] * 3
        aliases = {6: 0, 7: 1, 8: 2}
    scores = heads * length * (PREFIX + length)
    return pl.pallas_call(
        attention_kernel,
        grid=(heads // 2,),
        in_specs=in_specs,
        out_specs=[at_pair, at_kv, at_kv, pl.BlockSpec((2 * PREFIX, HD), lambda i: (0, i // pairs))],
        out_shape=[
            jax.ShapeDtypeStruct((length, wide), jnp.bfloat16),
            jax.ShapeDtypeStruct((length, kv_wide), jnp.bfloat16),
            jax.ShapeDtypeStruct((length, kv_wide), jnp.bfloat16),
            jax.ShapeDtypeStruct((2 * PREFIX, count * HD), jnp.bfloat16),
        ],
        scratch_shapes=[
            pltpu.VMEM((PREFIX + length, HD), jnp.bfloat16),
            pltpu.VMEM((PREFIX + length, HD), jnp.bfloat16),
            pltpu.VMEM((PREFIX + length, HD), jnp.float32),
            pltpu.VMEM((PREFIX + length, HD), jnp.float32),
        ],
        input_output_aliases=aliases,
        compiler_params=pltpu.CompilerParams(vmem_limit_bytes=32 << 20),
        cost_estimate=pl.CostEstimate(
            flops=10 * scores * HD,
            bytes_accessed=8 * length * heads * HD,
            transcendentals=scores,
        ),
    )(d_attn, queries, keys, values, prefix_keys, prefix_values, *held)


def sum_over(x, axis, size):
    step = 1
    while step < size:
        other = lax.ppermute(x, axis, [(i, i ^ step) for i in range(size)])
        total = x.astype(jnp.float32) + other.astype(jnp.float32)
        step *= 2
        x = total.astype(jnp.bfloat16) if step < size else total
    return x.astype(jnp.float32)


def gather_rows(x, axis, size):
    rows = x.shape[0]
    me = lax.axis_index(axis)
    if size == 2:
        other = lax.ppermute(x, axis, [(0, 1), (1, 0)])
        first = me == 0
        return jnp.concatenate([jnp.where(first, x, other), jnp.where(first, other, x)], 0)
    return lax.all_gather(x, axis, axis=0, tiled=True)


def shards(n_dp, n_tensor, grad_out, out_weight, queries, keys, values, prefix_keys, prefix_values):
    full_rows = gather_rows(grad_out, "tensor", n_tensor)
    kv_local = keys.shape[1] // HD
    wide = QH // KVH * HD
    parts = 2 if kv_local % 2 == 0 else 1
    count = kv_local // parts
    weights = [
        lax.all_gather(out_weight[c * count * wide : (c + 1) * count * wide], "dp", axis=1, tiled=True)
        for c in range(parts)
    ]
    held = ()
    sums = []
    for c in range(parts):
        weight = weights[c]
        if sums:
            weight, sums[-1] = lax.optimization_barrier((weight, sums[-1]))
        d_attn = dot(full_rows, weight, 1, 1).astype(jnp.bfloat16)
        *held, prefix = attention(c * count, d_attn, queries, keys, values, prefix_keys, prefix_values, held)
        sums.append(sum_over(prefix, "dp", n_dp))
    summed = jnp.concatenate(sums, axis=1)
    return (*held, summed[:PREFIX], summed[PREFIX:])


def solution(mesh):
    in_specs = (
        P(("dp", "tensor"), None),
        P("tensor", "dp"),
        P("dp", "tensor"),
        P("dp", "tensor"),
        P("dp", "tensor"),
        P(None, "tensor"),
        P(None, "tensor"),
    )
    out_specs = (
        P("dp", "tensor"),
        P("dp", "tensor"),
        P("dp", "tensor"),
        P(None, "tensor"),
        P(None, "tensor"),
    )
    body = functools.partial(shards, mesh.shape["dp"], mesh.shape["tensor"])
    return jax.shard_map(body, mesh=mesh, in_specs=in_specs, out_specs=out_specs, check_vma=False)
```
